32 devices in a mesh: row: 4 (over z), col: 8 (over y, x, core).
Axes of the slice: x: 2, y: 2, z: 4, core: 2. Of those that a mesh axis runs over, the one named last changes fastest.
Arguments:
- features: bfloat16 [131072, 128], P(('row', 'col')), may hold values from -6 to 6
- neighbors: int32 [131072, 10], P(('row', 'col')), may hold values from 0 to 7167, as said below
- counts: int32 [131072], P(('row', 'col')), may hold values from 1 to 10
- hub_rows: int32 [4096], P(('row', 'col')), may hold values from 0 to 4095, as said below
- w_self: bfloat16 [128, 256], replicated, may hold values from -0.5 to 0.5
- w_neigh: bfloat16 [128, 256], replicated, may hold values from -0.5 to 0.5
- out_bias: float32 [256], replicated, may hold values from -3 to 3
- cotangent: bfloat16 [131072, 256], P(('row', 'col')), may hold values from -6 to 6
Outputs:
- activations: bfloat16 [131072, 256], P(('row', 'col'))
- grad_features: bfloat16 [131072, 128], P(('row', 'col'))
- grad_w_self: float32 [128, 256], replicated
- grad_w_neigh: float32 [128, 256], replicated
- grad_bias: float32 [256], replicated
The draws below stay inside these ranges and needn't reach their ends.
Inputs may be any that keep to these rules, and one draw needn't show every extreme that they name: `neighbors`: rows below 1024 are never used by a partition of row 0, rows 5120 to 6143 never by one of the last row; slots at or past a node's count hold valid rows and are ignored. `hub_rows`: the 128 rows of one partition are distinct.
All inputs are finite; a program needn't handle non-finite values.
Results may differ from the reference program's by a relative error of at most 0.0075.
Values may be sent and summed in bfloat16 or wider, within the bound.
A program may use at most 256 MiB of HBM per device.

```python
import jax
import jax.numpy as jnp
from jax import lax

F = 128
H = 256
NODE_DEV = 4096
HUB_DEV = 128
FANOUT = 10
HALO = 1024
NODES = 131072
N_ROW = 4
N_COL = 8
DEVICES = 32


def draw_neighbors(key, part):
    key = jax.random.fold_in(key, 11)
    keys = jax.random.split(key, 5)
    total = NODE_DEV * DEVICES
    shape = (total, FANOUT)
    hub_count = HUB_DEV * N_COL
    extent = 2 * HALO + NODE_DEV + hub_count
    node = jnp.arange(total, dtype=jnp.int32)
    local_pos = node % NODE_DEV
    row_of = (node // NODE_DEV // N_COL)[:, None]
    category = jax.random.randint(keys[0], shape, 0, 20)
    inside = HALO + jax.random.randint(keys[1], shape, 0, NODE_DEV)
    border = jax.random.randint(keys[2], shape, 0, 2 * HALO)
    border = jnp.where((row_of == 0) & (border < HALO), border + HALO, border)
    border = jnp.where((row_of == N_ROW - 1) & (border >= HALO), border - HALO, border)
    border = jnp.where(border < HALO, border, border + NODE_DEV)
    first_hub = jax.random.randint(keys[3], shape, 0, hub_count)
    second_hub = jax.random.randint(keys[4], shape, 0, hub_count)
    hubward = 2 * HALO + NODE_DEV + jnp.minimum(first_hub, second_hub)
    picked = jnp.where(category < 14, inside, jnp.where(category < 17, border, hubward))
    leading = picked[:, 0]
    leading = jnp.where(local_pos == 0, extent - 1, jnp.where(local_pos == 1, HALO, jnp.where((local_pos == 2) & (row_of[:, 0] > 0), 0, leading)))
    return picked.at[:, 0].set(leading).astype(jnp.int32)


def draw_counts(key, part):
    key = jax.random.fold_in(key, 12)
    total = NODE_DEV * DEVICES
    node = jnp.arange(total, dtype=jnp.int32)
    drawn = jax.random.randint(key, (total,), 1, FANOUT + 1)
    drawn = jnp.where(node % 128 == 0, FANOUT, jnp.where(node % 128 == 1, 1, drawn))
    return drawn.astype(jnp.int32)


def draw_hub_rows(key, part):
    key = jax.random.fold_in(key, 13)
    total = DEVICES * HUB_DEV
    stride = NODE_DEV // HUB_DEV
    position = jnp.arange(total, dtype=jnp.int32) % HUB_DEV
    offsets = jax.random.randint(key, (total,), 0, stride)
    picked = position * stride + offsets
    picked = picked.at[0].set(0).at[HUB_DEV - 1].set(NODE_DEV - 1)
    return picked.astype(jnp.int32)


def block_levels(own_key, shape, cuts, least, largest):
    gain = 1.0
    for dim, shards_of in cuts:
        steps = jax.random.uniform(jax.random.fold_in(jax.random.fold_in(own_key, 6), dim), (shards_of,), jnp.float32, least / len(cuts), largest / len(cuts))
        gain = gain * jnp.repeat(jnp.exp(steps), shape[dim] // shards_of).reshape((-1,) + (1,) * (len(shape) - 1 - dim))
    return gain


def centred(own_key, shape, scale, bound, pieces=(), kind=jnp.bfloat16):
    values = jax.random.normal(own_key, shape, jnp.float32) * scale
    if len(pieces) > 0:
        values = block_levels(own_key, shape, pieces, -0.22, 0.18) * values
    return jnp.clip(values, min=-bound, max=bound).astype(kind)


def setup_inputs(seed: int = 0) -> dict:
    key_of = jax.random.split(jax.random.key(seed), 9)
    return {
        "features": centred(key_of[0], (NODES, F), 1.0, 6.0, ((0, 32),)),
        "neighbors": draw_neighbors(jax.random.fold_in(key_of[8], 71), 0),
        "counts": draw_counts(jax.random.fold_in(key_of[8], 71), 0),
        "hub_rows": draw_hub_rows(jax.random.fold_in(key_of[8], 71), 0),
        "w_self": centred(key_of[4], (F, H), F ** -0.5, 0.5),
        "w_neigh": centred(key_of[5], (F, H), F ** -0.5, 0.5),
        "out_bias": centred(key_of[6], (H,), 0.5, 3.0, (), jnp.float32),
        "cotangent": centred(key_of[7], (NODES, H), 1.0, 6.0, ((0, 32),)),
    }


def gelu_tanh(value):
    return jax.nn.gelu(value, approximate=True)

def reference(features, neighbors, counts, hub_rows, w_self, w_neigh, out_bias, cotangent):
    node_count = NODE_DEV
    extent = 2 * HALO + node_count + HUB_DEV * N_COL
    cube = features.reshape(N_ROW, N_COL, node_count, F)
    hub_index = hub_rows.reshape(N_ROW, N_COL, HUB_DEV)
    hub_table = jax.vmap(jax.vmap(lambda block, picks: jnp.take(block, picks, axis=0)))(cube, hub_index)
    hub_table = hub_table.reshape(N_ROW, N_COL * HUB_DEV, F)
    slot_ids = neighbors.reshape(DEVICES, node_count, FANOUT)
    live_counts = counts.reshape(DEVICES, node_count)
    cot_parts = cotangent.reshape(DEVICES, node_count, H)
    zero_rim = jnp.zeros((HALO, F), jnp.bfloat16)

    def per_partition(carry, inputs):
        index_part, slots, count_part, cot_part = inputs
        row_pos = index_part // N_COL
        col_pos = index_part % N_COL
        mine = cube[row_pos, col_pos]
        lower = jnp.where(row_pos > 0, cube[jnp.maximum(row_pos - 1, 0), col_pos, node_count - HALO:], zero_rim)
        upper = jnp.where(row_pos < N_ROW - 1, cube[jnp.minimum(row_pos + 1, N_ROW - 1), col_pos, :HALO], zero_rim)
        table = jnp.concatenate([lower, mine, upper, hub_table[row_pos]], axis=0)
        active = jnp.arange(FANOUT)[None, :] < count_part[:, None]
        divisor = count_part.astype(jnp.float32)[:, None]
        picked = table[slots].astype(jnp.float32)
        agg = (lax.optimization_barrier(jnp.sum(jnp.where(active[:, :, None], picked, 0.0), axis=1)) / divisor).astype(jnp.bfloat16)
        pre = jnp.dot(mine, w_self, preferred_element_type=jnp.float32) + jnp.dot(agg, w_neigh, preferred_element_type=jnp.float32) + out_bias.astype(jnp.float32)
        act, backward = jax.vjp(gelu_tanh, pre)
        dz = backward(cot_part.astype(jnp.float32))[0].astype(jnp.bfloat16)
        dims = (((0,), (0,)), ((), ()))
        grad_self = carry[0] + lax.dot_general(mine, dz, dims, preferred_element_type=jnp.float32)
        grad_neigh = carry[1] + lax.dot_general(agg, dz, dims, preferred_element_type=jnp.float32)
        grad_b = carry[2] + lax.optimization_barrier(jnp.sum(dz.astype(jnp.float32), axis=0))
        back_dims = (((1,), (1,)), ((), ()))
        d_agg = lax.dot_general(dz, w_neigh, back_dims, preferred_element_type=jnp.float32) / divisor
        values = jnp.where(active[:, :, None], d_agg[:, None, :], 0.0)
        d_table = jnp.zeros((extent, F), jnp.float32).at[slots.reshape(-1)].add(values.reshape(-1, F))
        base = lax.dot_general(dz, w_self, back_dims, preferred_element_type=jnp.float32) + d_table[HALO:HALO + node_count]
        outputs = (act.astype(jnp.bfloat16), base, d_table[:HALO], d_table[HALO + node_count:2 * HALO + node_count], d_table[2 * HALO + node_count:])
        return ((grad_self, grad_neigh, grad_b), outputs)
    init = (jnp.zeros((F, H), jnp.float32), jnp.zeros((F, H), jnp.float32), jnp.zeros((H,), jnp.float32))
    part_ids = jnp.arange(DEVICES, dtype=jnp.int32)
    sums, outputs = lax.scan(per_partition, init, (part_ids, slot_ids, live_counts, cot_parts))
    acts, base, lower_grads, upper_grads, hub_grads = outputs
    base = base.reshape(N_ROW, N_COL, node_count, F)
    lower_grads = lower_grads.reshape(N_ROW, N_COL, HALO, F)
    upper_grads = upper_grads.reshape(N_ROW, N_COL, HALO, F)
    zero_row = jnp.zeros((1, N_COL, HALO, F), jnp.float32)
    from_above = jnp.concatenate([zero_row, upper_grads[:-1]], axis=0)
    from_below = jnp.concatenate([lower_grads[1:], zero_row], axis=0)
    base = base.at[:, :, :HALO].add(from_above)
    base = base.at[:, :, node_count - HALO:].add(from_below)
    hub_total = lax.optimization_barrier(jnp.sum(hub_grads.reshape(N_ROW, N_COL, N_COL, HUB_DEV, F), axis=1))
    base = jax.vmap(jax.vmap(lambda block, picks, extra: block.at[picks].add(extra)))(base, hub_index, hub_total)
    grad_features = base.reshape(DEVICES * node_count, F).astype(jnp.bfloat16)
    activations = acts.reshape(DEVICES * node_count, H)
    return (activations, grad_features, sums[0], sums[1], sums[2])
```

```python
import functools

import jax
import jax.numpy as jnp
from jax import lax
from jax.experimental import pallas as pl
from jax.experimental.pallas import tpu as pltpu
from jax.sharding import PartitionSpec as P

FANOUT = 10
HALO = 1024
UNROLL = 8
PAD = 8
VMEM_LIMIT = 60 * 1024 * 1024


def gather_kernel(rows_ref, lower_ref, own_ref, upper_ref, hub_ref, total_ref, table):
    at = 0
    for part in (lower_ref, own_ref, upper_ref, hub_ref):
        size = part.shape[0]
        table[at : at + size, :] = part[...].astype(jnp.float32)
        at += size
    table[at : at + PAD, :] = jnp.zeros((PAD, table.shape[1]), jnp.float32)

    def step(i, carry):
        for u in range(UNROLL):
            n = i * UNROLL + u
            picked = [table[pl.ds(rows_ref[s, n], 1), :] for s in range(FANOUT)]
            while len(picked) > 1:
                picked = [a + b for a, b in zip(picked[::2], picked[1::2])] + (
                    [picked[-1]] if len(picked) % 2 else []
                )
            total_ref[pl.ds(n, 1), :] = picked[0]
        return carry

    lax.fori_loop(0, total_ref.shape[0] // UNROLL, step, 0)


def gather_sum(rows, lower, own, upper, hubs):
    extent = lower.shape[0] + own.shape[0] + upper.shape[0] + hubs.shape[0]
    vmem = pl.BlockSpec(memory_space=pltpu.VMEM)
    return pl.pallas_call(
        gather_kernel,
        out_shape=jax.ShapeDtypeStruct(own.shape, jnp.float32),
        in_specs=[pl.BlockSpec(memory_space=pltpu.SMEM)] + [vmem] * 4,
        out_specs=vmem,
        scratch_shapes=[pltpu.VMEM((extent + PAD, own.shape[1]), jnp.float32)],
        compiler_params=pltpu.CompilerParams(vmem_limit_bytes=VMEM_LIMIT),
        name="gather_sum",
    )(rows, lower, own, upper, hubs)


def scatter_kernel(rows_ref, source_ref, own_ref, border_ref, hub_ref, *sums):
    chunk = 512
    extent = sums[0].shape[0]
    width = sums[0].shape[1]
    kinds = len(sums)

    def clear(i, carry):
        for total in sums:
            total[pl.ds(pl.multiple_of(i * chunk, chunk), chunk), :] = jnp.zeros(
                (chunk, width), jnp.float32
            )
        return carry

    lax.fori_loop(0, extent // chunk, clear, 0)

    def step(i, carry):
        for u in range(UNROLL):
            n = i * UNROLL + u
            value = source_ref[pl.ds(n, 1), :]
            for first in range(0, FANOUT, kinds):
                rows = [rows_ref[first + k, n] for k in range(kinds)]
                held = [sums[k][pl.ds(rows[k], 1), :] for k in range(kinds)]
                for k in range(kinds):
                    sums[k][pl.ds(rows[k], 1), :] = held[k] + value
        return carry

    lax.fori_loop(0, source_ref.shape[0] // UNROLL, step, 0)

    def added(at, size):
        total = sums[0][pl.ds(at, size), :]
        for other in sums[1:]:
            total = total + other[pl.ds(at, size), :]
        return total

    def emit(ref, ref_at, at, count):
        def one(i, carry):
            off = pl.multiple_of(i * 128, 128)
            ref[pl.ds(ref_at + off, 128), :] = added(at + off, 128).astype(ref.dtype)
            return carry

        lax.fori_loop(0, count // 128, one, 0)

    nodes = own_ref.shape[0]
    emit(border_ref, 0, 0, HALO)
    emit(own_ref, 0, HALO, nodes)
    emit(border_ref, HALO, HALO + nodes, HALO)
    emit(hub_ref, 0, 2 * HALO + nodes, hub_ref.shape[0])


def scatter_sum(rows, source, hubs):
    nodes, width = source.shape
    extent = 2 * HALO + nodes + hubs
    kinds = 10 if extent <= 8192 else 5
    vmem = pl.BlockSpec(memory_space=pltpu.VMEM)
    return pl.pallas_call(
        scatter_kernel,
        out_shape=(
            jax.ShapeDtypeStruct((nodes, width), jnp.float32),
            jax.ShapeDtypeStruct((2 * HALO, width), jnp.bfloat16),
            jax.ShapeDtypeStruct((hubs, width), jnp.bfloat16),
        ),
        in_specs=[pl.BlockSpec(memory_space=pltpu.SMEM), vmem],
        out_specs=(vmem, vmem, vmem),
        scratch_shapes=[pltpu.VMEM((extent + PAD, width), jnp.float32)] * kinds,
        compiler_params=pltpu.CompilerParams(vmem_limit_bytes=VMEM_LIMIT),
        name="scatter_sum",
    )(rows, source)


def rims(head, tail, axis):
    count = lax.axis_size(axis)
    ends = count - 1
    return (
        lax.ppermute(tail, axis, [(i, i + 1) for i in range(ends)]),
        lax.ppermute(head, axis, [(i + 1, i) for i in range(ends)]),
    )


def gelu_tanh(value):
    return jax.nn.gelu(value, approximate=True)


def on_device(features, neighbors, counts, hub_rows, w_self, w_neigh, out_bias, cotangent):
    node_count = features.shape[0]
    lower, upper = rims(features[:HALO], features[node_count - HALO :], "row")
    hub_local = jnp.take(features, hub_rows, axis=0)
    hub_table = lax.all_gather(hub_local, "col", axis=0, tiled=True)
    hubs = hub_table.shape[0]
    extent = 2 * HALO + node_count + hubs
    active = jnp.arange(FANOUT)[:, None] < counts[None, :]
    rows = jnp.where(active, neighbors.T, extent)
    divisor = counts.astype(jnp.float32)[:, None]
    agg = (gather_sum(rows, lower, features, upper, hub_table) / divisor).astype(jnp.bfloat16)
    pre = (
        jnp.dot(features, w_self, preferred_element_type=jnp.float32)
        + jnp.dot(agg, w_neigh, preferred_element_type=jnp.float32)
        + out_bias
    )
    act, backward = jax.vjp(gelu_tanh, pre)
    activations = act.astype(jnp.bfloat16)
    dz = backward(cotangent.astype(jnp.float32))[0].astype(jnp.bfloat16)
    dims = (((0,), (0,)), ((), ()))
    back_dims = (((1,), (1,)), ((), ()))
    grad_self = lax.dot_general(features, dz, dims, preferred_element_type=jnp.float32)
    grad_b = jnp.sum(dz.astype(jnp.float32), axis=0)
    grad_neigh = lax.dot_general(agg, dz, dims, preferred_element_type=jnp.float32)
    source = lax.dot_general(dz, w_neigh, back_dims, preferred_element_type=jnp.float32) / divisor
    mine, border, hub_grads = scatter_sum(rows, source, hubs)
    from_above, from_below = rims(border[:HALO], border[HALO:], "row")
    mine = mine.at[:HALO].add(from_above.astype(jnp.float32))
    mine = mine.at[node_count - HALO :].add(from_below.astype(jnp.float32))
    hub_share = lax.psum_scatter(hub_grads, "col", scatter_dimension=0, tiled=True).astype(
        jnp.float32
    )
    mine = mine.at[hub_rows].add(hub_share)
    local_grad = lax.dot_general(dz, w_self, back_dims, preferred_element_type=jnp.float32)
    grad_features = (local_grad + mine).astype(jnp.bfloat16)
    grad_self, grad_neigh, grad_b = lax.psum((grad_self, grad_neigh, grad_b), ("row", "col"))
    return (activations, grad_features, grad_self, grad_neigh, grad_b)


def solution(mesh):
    placed = (
        P(("row", "col"), None),
        P(("row", "col"), None),
        P(("row", "col")),
        P(("row", "col")),
        P(),
        P(),
        P(),
        P(("row", "col"), None),
    )
    return jax.shard_map(
        on_device,
        mesh=mesh,
        in_specs=placed,
        out_specs=(P(("row", "col"), None), P(("row", "col"), None), P(), P(), P()),
        check_vma=False,
    )
```

```python
import functools

import jax
import jax.numpy as jnp
from jax import lax
from jax.experimental import pallas as pl
from jax.experimental.pallas import tpu as pltpu
from jax.sharding import PartitionSpec as P

FANOUT = 10
HALO = 1024
UNROLL = 8
PAD = 8
VMEM_LIMIT = 60 * 1024 * 1024


def gather_kernel(rows_ref, lower_ref, own_ref, upper_ref, hub_ref, total_ref, table):
    at = 0
    for part in (lower_ref, own_ref, upper_ref, hub_ref):
        size = part.shape[0]
        table[at : at + size, :] = part[...].astype(jnp.float32)
        at += size
    table[at : at + PAD, :] = jnp.zeros((PAD, table.shape[1]), jnp.float32)

    def step(i, carry):
        for u in range(UNROLL):
            n = i * UNROLL + u
            picked = [table[pl.ds(rows_ref[s, n], 1), :] for s in range(FANOUT)]
            while len(picked) > 1:
                picked = [a + b for a, b in zip(picked[::2], picked[1::2])] + (
                    [picked[-1]] if len(picked) % 2 else []
                )
            total_ref[pl.ds(n, 1), :] = picked[0]
        return carry

    lax.fori_loop(0, total_ref.shape[0] // UNROLL, step, 0)


def gather_sum(rows, lower, own, upper, hubs):
    extent = lower.shape[0] + own.shape[0] + upper.shape[0] + hubs.shape[0]
    vmem = pl.BlockSpec(memory_space=pltpu.VMEM)
    return pl.pallas_call(
        gather_kernel,
        out_shape=jax.ShapeDtypeStruct(own.shape, jnp.float32),
        in_specs=[pl.BlockSpec(memory_space=pltpu.SMEM)] + [vmem] * 4,
        out_specs=vmem,
        scratch_shapes=[pltpu.VMEM((extent + PAD, own.shape[1]), jnp.float32)],
        compiler_params=pltpu.CompilerParams(vmem_limit_bytes=VMEM_LIMIT),
        name="gather_sum",
    )(rows, lower, own, upper, hubs)


def scatter_kernel(rows_ref, source_ref, own_ref, border_ref, hub_ref, *sums):
    chunk = 512
    extent = sums[0].shape[0]
    width = sums[0].shape[1]
    kinds = len(sums)

    def clear(i, carry):
        for total in sums:
            total[pl.ds(pl.multiple_of(i * chunk, chunk), chunk), :] = jnp.zeros(
                (chunk, width), jnp.float32
            )
        return carry

    lax.fori_loop(0, extent // chunk, clear, 0)

    def step(i, carry):
        for u in range(UNROLL):
            n = i * UNROLL + u
            value = source_ref[pl.ds(n, 1), :]
            for first in range(0, FANOUT, kinds):
                rows = [rows_ref[first + k, n] for k in range(kinds)]
                held = [sums[k][pl.ds(rows[k], 1), :] for k in range(kinds)]
                for k in range(kinds):
                    sums[k][pl.ds(rows[k], 1), :] = held[k] + value
        return carry

    lax.fori_loop(0, source_ref.shape[0] // UNROLL, step, 0)

    def added(at, size):
        total = sums[0][pl.ds(at, size), :]
        for other in sums[1:]:
            total = total + other[pl.ds(at, size), :]
        return total

    def emit(ref, ref_at, at, count):
        def one(i, carry):
            off = pl.multiple_of(i * 128, 128)
            ref[pl.ds(ref_at + off, 128), :] = added(at + off, 128).astype(ref.dtype)
            return carry

        lax.fori_loop(0, count // 128, one, 0)

    nodes = own_ref.shape[0]
    emit(border_ref, 0, 0, HALO)
    emit(own_ref, 0, HALO, nodes)
    emit(border_ref, HALO, HALO + nodes, HALO)
    emit(hub_ref, 0, 2 * HALO + nodes, hub_ref.shape[0])


def scatter_sum(rows, source, hubs):
    nodes, width = source.shape
    extent = 2 * HALO + nodes + hubs
    kinds = 10 if extent <= 8192 else 5
    vmem = pl.BlockSpec(memory_space=pltpu.VMEM)
    return pl.pallas_call(
        scatter_kernel,
        out_shape=(
            jax.ShapeDtypeStruct((nodes, width), jnp.float32),
            jax.ShapeDtypeStruct((2 * HALO, width), jnp.bfloat16),
            jax.ShapeDtypeStruct((hubs, width), jnp.bfloat16),
        ),
        in_specs=[pl.BlockSpec(memory_space=pltpu.SMEM), vmem],
        out_specs=(vmem, vmem, vmem),
        scratch_shapes=[pltpu.VMEM((extent + PAD, width), jnp.float32)] * kinds,
        compiler_params=pltpu.CompilerParams(vmem_limit_bytes=VMEM_LIMIT),
        name="scatter_sum",
    )(rows, source)


MESH = pl.DeviceIdType.MESH


def greet(row, col, row_peers, col_peers):
    barrier = pltpu.get_barrier_semaphore()
    for peer in row_peers:
        pl.semaphore_signal(barrier, inc=1, device_id=(peer, col), device_id_type=MESH)
    for peer in col_peers:
        pl.semaphore_signal(barrier, inc=1, device_id=(row, peer), device_id_type=MESH)
    pl.semaphore_wait(barrier, len(row_peers) + len(col_peers))


def rim_copies(row, col, n_row, head, tail, below, above, send, recv):
    up = pltpu.make_async_remote_copy(
        src_ref=tail,
        dst_ref=above,
        send_sem=send.at[0],
        recv_sem=recv.at[0],
        device_id=(lax.rem(row + 1, n_row), col),
        device_id_type=MESH,
    )
    down = pltpu.make_async_remote_copy(
        src_ref=head,
        dst_ref=below,
        send_sem=send.at[1],
        recv_sem=recv.at[1],
        device_id=(lax.rem(row + n_row - 1, n_row), col),
        device_id_type=MESH,
    )
    return up, down


def start_rims(row, n_row, up, down):
    pl.when(row < n_row - 1)(lambda: up.start())
    pl.when(row > 0)(lambda: down.start())


def finish_rims(row, n_row, up, down):
    @pl.when(row < n_row - 1)
    def _():
        up.wait_send()
        down.wait_recv()

    @pl.when(row > 0)
    def _():
        down.wait_send()
        up.wait_recv()


def entry_kernel(
    n_row, n_col, own, hub, lower, upper, hubs, own_sem, rim_send, rim_recv, hub_send, hub_recv
):
    row, col = lax.axis_index("row"), lax.axis_index("col")
    nodes, share = own.shape[0], hub.shape[0]
    peers = [lax.rem(col + k, n_col) for k in range(1, n_col)]
    greet(row, col, [lax.rem(row + k, n_row) for k in range(1, n_row)], peers)
    up, down = rim_copies(
        row,
        col,
        n_row,
        own.at[pl.ds(0, HALO)],
        own.at[pl.ds(nodes - HALO, HALO)],
        upper,
        lower,
        rim_send,
        rim_recv,
    )
    start_rims(row, n_row, up, down)
    mine = hubs.at[pl.ds(pl.multiple_of(col * share, share), share)]
    copies = [
        pltpu.make_async_remote_copy(
            src_ref=hub,
            dst_ref=mine,
            send_sem=hub_send.at[k],
            recv_sem=hub_recv.at[k],
            device_id=(row, peer),
            device_id_type=MESH,
        )
        for k, peer in enumerate(peers)
    ]
    for copy in copies:
        copy.start()
    kept = pltpu.make_async_copy(hub, mine, own_sem)
    kept.start()
    kept.wait()
    for copy in copies:
        copy.wait()
    finish_rims(row, n_row, up, down)


def entry_exchange(features, hub_local, n_row, n_col):
    width = features.shape[1]
    share = hub_local.shape[0]
    anywhere = pl.BlockSpec(memory_space=pl.ANY)
    dma = pltpu.SemaphoreType.DMA
    return pl.pallas_call(
        functools.partial(entry_kernel, n_row, n_col),
        out_shape=(
            jax.ShapeDtypeStruct((HALO, width), jnp.bfloat16),
            jax.ShapeDtypeStruct((HALO, width), jnp.bfloat16),
            jax.ShapeDtypeStruct((n_col * share, width), jnp.bfloat16),
        ),
        in_specs=[anywhere] * 2,
        out_specs=(anywhere,) * 3,
        scratch_shapes=[dma, dma((2,)), dma((2,)), dma((n_col - 1,)), dma((n_col - 1,))],
        compiler_params=pltpu.CompilerParams(collective_id=0, has_side_effects=True),
        name="entry_exchange",
    )(features, hub_local)


def exit_kernel(
    n_row,
    n_col,
    border,
    hub,
    grads,
    rim,
    hub_total,
    weights,
    bias,
    hub_in,
    col_in,
    row_in,
    rim_send,
    rim_recv,
    hub_send,
    hub_recv,
    col_send,
    col_recv,
    row_send,
    row_recv,
    out_send,
    out_recv,
):
    row, col = lax.axis_index("row"), lax.axis_index("col")
    share = hub_total.shape[0]
    part = weights.shape[1]
    peers = [lax.rem(col + k, n_col) for k in range(1, n_col)]
    row_peers = [lax.rem(row + k, n_row) for k in range(1, n_row)]
    greet(row, col, row_peers, peers)

    def remote(src, dst, send, recv, device):
        return pltpu.make_async_remote_copy(
            src_ref=src,
            dst_ref=dst,
            send_sem=send,
            recv_sem=recv,
            device_id=device,
            device_id_type=MESH,
        )

    first = [
        remote(grads.at[peer], col_in.at[col], col_send.at[k], col_recv.at[k], (row, peer))
        for k, peer in enumerate(peers)
    ]
    for copy in first:
        copy.start()
    up, down = rim_copies(
        row,
        col,
        n_row,
        border.at[pl.ds(0, HALO)],
        border.at[pl.ds(HALO, HALO)],
        rim.at[pl.ds(HALO, HALO)],
        rim.at[pl.ds(0, HALO)],
        rim_send,
        rim_recv,
    )
    start_rims(row, n_row, up, down)
    sends = [
        remote(
            hub.at[pl.ds(pl.multiple_of(peer * share, share), share)],
            hub_in.at[col],
            hub_send.at[k],
            hub_recv.at[k],
            (row, peer),
        )
        for k, peer in enumerate(peers)
    ]
    for copy in sends:
        copy.start()

    @pl.when(row == 0)
    def _():
        rim[:HALO, :] = jnp.zeros((HALO, rim.shape[1]), rim.dtype)

    @pl.when(row == n_row - 1)
    def _():
        rim[HALO:, :] = jnp.zeros((HALO, rim.shape[1]), rim.dtype)

    col_in[col] = grads[col]
    for copy in first:
        copy.wait()
    total = col_in[0]
    for k in range(1, n_col):
        total = total + col_in[k]
    row_in[row] = total
    second = [
        remote(row_in.at[row], row_in.at[row], row_send.at[k], row_recv.at[k], (peer, col))
        for k, peer in enumerate(row_peers)
    ]
    for copy in second:
        copy.start()
    hub_in[col] = hub[pl.ds(pl.multiple_of(col * share, share), share), :]
    for copy in second:
        copy.wait()
    total = row_in[0]
    for k in range(1, n_row):
        total = total + row_in[k]
    weights[col] = total[:part]
    bias[...] = jnp.sum(total[part:], axis=0, keepdims=True)
    third = [
        remote(weights.at[col], weights.at[col], out_send.at[k], out_recv.at[k], (row, peer))
        for k, peer in enumerate(peers)
    ]
    for copy in third:
        copy.start()
    for copy in sends:
        copy.wait()
    shared = hub_in[0].astype(jnp.float32)
    for k in range(1, n_col):
        shared = shared + hub_in[k].astype(jnp.float32)
    hub_total[...] = shared
    for copy in third:
        copy.wait()
    finish_rims(row, n_row, up, down)


def exit_exchange(border, hub, grads, n_row, n_col):
    width = border.shape[1]
    share = hub.shape[0] // n_col
    part, hidden = grads.shape[1] - 8, grads.shape[2]
    vmem = pl.BlockSpec(memory_space=pltpu.VMEM)
    dma = pltpu.SemaphoreType.DMA
    return pl.pallas_call(
        functools.partial(exit_kernel, n_row, n_col),
        out_shape=(
            jax.ShapeDtypeStruct(border.shape, jnp.bfloat16),
            jax.ShapeDtypeStruct((share, width), jnp.float32),
            jax.ShapeDtypeStruct((n_col, part, hidden), jnp.float32),
            jax.ShapeDtypeStruct((1, hidden), jnp.float32),
        ),
        in_specs=[vmem] * 3,
        out_specs=(vmem,) * 4,
        scratch_shapes=[
            pltpu.VMEM((n_col, share, width), jnp.bfloat16),
            pltpu.VMEM(grads.shape, jnp.float32),
            pltpu.VMEM((n_row,) + grads.shape[1:], jnp.float32),
            dma((2,)),
            dma((2,)),
        ]
        + [dma((n_col - 1,))] * 4
        + [dma((n_row - 1,))] * 2
        + [dma((n_col - 1,))] * 2,
        compiler_params=pltpu.CompilerParams(
            collective_id=1, has_side_effects=True, vmem_limit_bytes=VMEM_LIMIT
        ),
        name="exit_exchange",
    )(border, hub, grads)


def finish_kernel(hub_rows, own, dz, w_self, rim, hub, out, total):
    chunk = 512
    nodes = own.shape[0]

    def back(i, carry):
        at = pl.ds(pl.multiple_of(i * chunk, chunk), chunk)
        total[at, :] = own[at, :] + lax.dot_general(
            dz[at, :], w_self[...], (((1,), (1,)), ((), ())), preferred_element_type=jnp.float32
        )
        return carry

    lax.fori_loop(0, nodes // chunk, back, 0)
    total[:HALO, :] += rim[:HALO, :].astype(jnp.float32)
    total[nodes - HALO :, :] += rim[HALO:, :].astype(jnp.float32)

    def add(i, carry):
        for u in range(UNROLL):
            k = i * UNROLL + u
            at = pl.ds(hub_rows[k], 1)
            total[at, :] += hub[pl.ds(k, 1), :]
        return carry

    lax.fori_loop(0, hub.shape[0] // UNROLL, add, 0)
    out[...] = total[...].astype(out.dtype)


def finish(hub_rows, own, dz, w_self, rim, hub):
    vmem = pl.BlockSpec(memory_space=pltpu.VMEM)
    return pl.pallas_call(
        finish_kernel,
        out_shape=jax.ShapeDtypeStruct(own.shape, jnp.bfloat16),
        in_specs=[pl.BlockSpec(memory_space=pltpu.SMEM)] + [vmem] * 5,
        out_specs=vmem,
        scratch_shapes=[pltpu.VMEM(own.shape, jnp.float32)],
        compiler_params=pltpu.CompilerParams(vmem_limit_bytes=VMEM_LIMIT),
        name="finish",
    )(hub_rows, own, dz, w_self, rim, hub)


def gelu_tanh(value):
    return jax.nn.gelu(value, approximate=True)


def on_device(features, neighbors, counts, hub_rows, w_self, w_neigh, out_bias, cotangent):
    node_count = features.shape[0]
    n_row, n_col = lax.axis_size("row"), lax.axis_size("col")
    hub_local = jnp.take(features, hub_rows, axis=0)
    lower, upper, hub_table = entry_exchange(features, hub_local, n_row, n_col)
    hubs = hub_table.shape[0]
    extent = 2 * HALO + node_count + hubs
    active = jnp.arange(FANOUT)[:, None] < counts[None, :]
    rows = jnp.where(active, neighbors.T, extent)
    divisor = counts.astype(jnp.float32)[:, None]
    agg = (gather_sum(rows, lower, features, upper, hub_table) / divisor).astype(jnp.bfloat16)
    pre = (
        jnp.dot(features, w_self, preferred_element_type=jnp.float32)
        + jnp.dot(agg, w_neigh, preferred_element_type=jnp.float32)
        + out_bias
    )
    act, backward = jax.vjp(gelu_tanh, pre)
    activations = act.astype(jnp.bfloat16)
    dz = backward(cotangent.astype(jnp.float32))[0].astype(jnp.bfloat16)
    dims = (((0,), (0,)), ((), ()))
    back_dims = (((1,), (1,)), ((), ()))
    grad_self = lax.dot_general(features, dz, dims, preferred_element_type=jnp.float32)
    grad_b = jnp.sum(dz.astype(jnp.float32), axis=0)
    grad_neigh = lax.dot_general(agg, dz, dims, preferred_element_type=jnp.float32)
    source = lax.dot_general(dz, w_neigh, back_dims, preferred_element_type=jnp.float32) / divisor
    mine, border, hub_grads = scatter_sum(rows, source, hubs)
    hidden = dz.shape[1]
    blocks = jnp.concatenate([grad_self, grad_neigh], axis=0).reshape(n_col, -1, hidden)
    grads = jnp.concatenate([blocks, jnp.broadcast_to(jnp.pad(grad_b[None, :], ((0, 7), (0, 0))), (n_col, 8, hidden))], axis=1)
    rim, hub_share, weights, bias = exit_exchange(border, hub_grads, grads, n_row, n_col)
    grad_features = finish(hub_rows, mine, dz, w_self, rim, hub_share)
    weights = weights.reshape(2, -1, hidden)
    grad_self, grad_neigh, grad_b = weights[0], weights[1], bias[0]
    return (activations, grad_features, grad_self, grad_neigh, grad_b)


def solution(mesh):
    placed = (
        P(("row", "col"), None),
        P(("row", "col"), None),
        P(("row", "col")),
        P(("row", "col")),
        P(),
        P(),
        P(),
        P(("row", "col"), None),
    )
    return jax.shard_map(
        on_device,
        mesh=mesh,
        in_specs=placed,
        out_specs=(P(("row", "col"), None), P(("row", "col"), None), P(), P(), P()),
        check_vma=False,
    )
```

```python
import functools

import jax
import jax.numpy as jnp
from jax import lax
from jax.experimental import pallas as pl
from jax.experimental.pallas import tpu as pltpu
from jax.sharding import PartitionSpec as P

FANOUT = 10
HALO = 1024
UNROLL = 8
VMEM_LIMIT = 60 * 1024 * 1024


def by_count(starts_ref, order_ref, visit):
    for live in range(1, FANOUT + 1):
        first, last = starts_ref[live - 1], starts_ref[live]
        groups = lax.div(last - first, UNROLL)

        def group(i, carry, first=first, live=live):
            at = first + i * UNROLL
            visit([order_ref[at + u] for u in range(UNROLL)], live)
            return carry

        def single(i, carry, live=live):
            visit([order_ref[i]], live)
            return carry

        lax.fori_loop(0, groups, group, 0)
        lax.fori_loop(first + groups * UNROLL, last, single, 0)


def gather_kernel(
    rows_ref, starts_ref, order_ref, lower_ref, own_ref, upper_ref, hub_ref, total_ref, table
):
    at = 0
    for part in (lower_ref, own_ref, upper_ref, hub_ref):
        size = part.shape[0]
        table[at : at + size, :] = part[...].astype(jnp.float32)
        at += size

    def visit(nodes, live):
        for n in nodes:
            picked = [table[pl.ds(rows_ref[s, n], 1), :] for s in range(live)]
            while len(picked) > 1:
                picked = [a + b for a, b in zip(picked[::2], picked[1::2])] + (
                    [picked[-1]] if len(picked) % 2 else []
                )
            total_ref[pl.ds(n, 1), :] = picked[0]

    by_count(starts_ref, order_ref, visit)


def gather_sum(rows, starts, order, lower, own, upper, hubs):
    extent = lower.shape[0] + own.shape[0] + upper.shape[0] + hubs.shape[0]
    vmem = pl.BlockSpec(memory_space=pltpu.VMEM)
    return pl.pallas_call(
        gather_kernel,
        out_shape=jax.ShapeDtypeStruct(own.shape, jnp.float32),
        in_specs=[pl.BlockSpec(memory_space=pltpu.SMEM)] * 3 + [vmem] * 4,
        out_specs=vmem,
        scratch_shapes=[pltpu.VMEM((extent, own.shape[1]), jnp.float32)],
        compiler_params=pltpu.CompilerParams(vmem_limit_bytes=VMEM_LIMIT),
        name="gather_sum",
    )(rows, starts, order, lower, own, upper, hubs)


def scatter_kernel(rows_ref, starts_ref, order_ref, source_ref, own_ref, border_ref, hub_ref, *sums):
    chunk = 512
    extent = sums[0].shape[0]
    width = sums[0].shape[1]
    kinds = len(sums)

    def clear(i, carry):
        for total in sums:
            total[pl.ds(pl.multiple_of(i * chunk, chunk), chunk), :] = jnp.zeros(
                (chunk, width), jnp.float32
            )
        return carry

    lax.fori_loop(0, extent // chunk, clear, 0)

    def visit(nodes, live):
        values = [source_ref[pl.ds(n, 1), :] for n in nodes]
        edges = [(u, s) for u in range(len(nodes)) for s in range(live)]
        for first in range(0, len(edges), kinds):
            batch = edges[first : first + kinds]
            rows = [rows_ref[s, nodes[u]] for u, s in batch]
            held = [sums[k][pl.ds(row, 1), :] for k, row in enumerate(rows)]
            for k, (u, s) in enumerate(batch):
                sums[k][pl.ds(rows[k], 1), :] = held[k] + values[u]

    by_count(starts_ref, order_ref, visit)

    def added(at, size):
        total = sums[0][pl.ds(at, size), :]
        for other in sums[1:]:
            total = total + other[pl.ds(at, size), :]
        return total

    def emit(ref, ref_at, at, count):
        def one(i, carry):
            off = pl.multiple_of(i * 128, 128)
            ref[pl.ds(ref_at + off, 128), :] = added(at + off, 128).astype(ref.dtype)
            return carry

        lax.fori_loop(0, count // 128, one, 0)

    nodes = own_ref.shape[0]
    emit(border_ref, 0, 0, HALO)
    emit(own_ref, 0, HALO, nodes)
    emit(border_ref, HALO, HALO + nodes, HALO)
    emit(hub_ref, 0, 2 * HALO + nodes, hub_ref.shape[0])


def scatter_sum(rows, starts, order, source, hubs):
    nodes, width = source.shape
    extent = 2 * HALO + nodes + hubs
    kinds = 10 if extent <= 8192 else 5
    vmem = pl.BlockSpec(memory_space=pltpu.VMEM)
    return pl.pallas_call(
        scatter_kernel,
        out_shape=(
            jax.ShapeDtypeStruct((nodes, width), jnp.float32),
            jax.ShapeDtypeStruct((2 * HALO, width), jnp.bfloat16),
            jax.ShapeDtypeStruct((hubs, width), jnp.bfloat16),
        ),
        in_specs=[pl.BlockSpec(memory_space=pltpu.SMEM)] * 3 + [vmem],
        out_specs=(vmem, vmem, vmem),
        scratch_shapes=[pltpu.VMEM((extent, width), jnp.float32)] * kinds,
        compiler_params=pltpu.CompilerParams(vmem_limit_bytes=VMEM_LIMIT),
        name="scatter_sum",
    )(rows, starts, order, source)


MESH = pl.DeviceIdType.MESH


def greet(row, col, row_peers, col_peers):
    barrier = pltpu.get_barrier_semaphore()
    for peer in row_peers:
        pl.semaphore_signal(barrier, inc=1, device_id=(peer, col), device_id_type=MESH)
    for peer in col_peers:
        pl.semaphore_signal(barrier, inc=1, device_id=(row, peer), device_id_type=MESH)
    pl.semaphore_wait(barrier, len(row_peers) + len(col_peers))


def rim_copies(row, col, n_row, head, tail, below, above, send, recv):
    up = pltpu.make_async_remote_copy(
        src_ref=tail,
        dst_ref=above,
        send_sem=send.at[0],
        recv_sem=recv.at[0],
        device_id=(lax.rem(row + 1, n_row), col),
        device_id_type=MESH,
    )
    down = pltpu.make_async_remote_copy(
        src_ref=head,
        dst_ref=below,
        send_sem=send.at[1],
        recv_sem=recv.at[1],
        device_id=(lax.rem(row + n_row - 1, n_row), col),
        device_id_type=MESH,
    )
    return up, down


def start_rims(row, n_row, up, down):
    pl.when(row < n_row - 1)(lambda: up.start())
    pl.when(row > 0)(lambda: down.start())


def finish_rims(row, n_row, up, down):
    @pl.when(row < n_row - 1)
    def _():
        up.wait_send()
        down.wait_recv()

    @pl.when(row > 0)
    def _():
        down.wait_send()
        up.wait_recv()


def entry_kernel(
    n_row,
    n_col,
    hub_rows,
    own,
    lower,
    upper,
    hubs,
    wide,
    picked,
    hub,
    own_sem,
    rim_send,
    rim_recv,
    hub_send,
    hub_recv,
):
    row, col = lax.axis_index("row"), lax.axis_index("col")
    nodes, share = own.shape[0], hub.shape[0]
    peers = [lax.rem(col + k, n_col) for k in range(1, n_col)]
    greet(row, col, [lax.rem(row + k, n_row) for k in range(1, n_row)], peers)
    up, down = rim_copies(
        row,
        col,
        n_row,
        own.at[pl.ds(0, HALO)],
        own.at[pl.ds(nodes - HALO, HALO)],
        upper,
        lower,
        rim_send,
        rim_recv,
    )
    start_rims(row, n_row, up, down)
    wide[...] = own[...].astype(jnp.float32)

    def pick(i, carry):
        for u in range(UNROLL):
            k = i * UNROLL + u
            picked[pl.ds(k, 1), :] = wide[pl.ds(hub_rows[k], 1), :]
        return carry

    lax.fori_loop(0, share // UNROLL, pick, 0)
    hub[...] = picked[...].astype(jnp.bfloat16)
    mine = hubs.at[pl.ds(pl.multiple_of(col * share, share), share)]
    copies = [
        pltpu.make_async_remote_copy(
            src_ref=hub,
            dst_ref=mine,
            send_sem=hub_send.at[k],
            recv_sem=hub_recv.at[k],
            device_id=(row, peer),
            device_id_type=MESH,
        )
        for k, peer in enumerate(peers)
    ]
    for copy in copies:
        copy.start()
    kept = pltpu.make_async_copy(hub, mine, own_sem)
    kept.start()
    kept.wait()
    for copy in copies:
        copy.wait()
    finish_rims(row, n_row, up, down)


def entry_exchange(features, hub_rows, n_row, n_col):
    width = features.shape[1]
    share = hub_rows.shape[0]
    anywhere = pl.BlockSpec(memory_space=pl.ANY)
    dma = pltpu.SemaphoreType.DMA
    return pl.pallas_call(
        functools.partial(entry_kernel, n_row, n_col),
        out_shape=(
            jax.ShapeDtypeStruct((HALO, width), jnp.bfloat16),
            jax.ShapeDtypeStruct((HALO, width), jnp.bfloat16),
            jax.ShapeDtypeStruct((n_col * share, width), jnp.bfloat16),
        ),
        in_specs=[
            pl.BlockSpec(memory_space=pltpu.SMEM),
            pl.BlockSpec(memory_space=pltpu.VMEM),
        ],
        out_specs=(anywhere,) * 3,
        scratch_shapes=[
            pltpu.VMEM(features.shape, jnp.float32),
            pltpu.VMEM((share, width), jnp.float32),
            pltpu.VMEM((share, width), jnp.bfloat16),
            dma,
            dma((2,)),
            dma((2,)),
            dma((n_col - 1,)),
            dma((n_col - 1,)),
        ],
        compiler_params=pltpu.CompilerParams(
            collective_id=0, has_side_effects=True, vmem_limit_bytes=VMEM_LIMIT
        ),
        name="entry_exchange",
    )(hub_rows, features)


def exit_kernel(
    n_row,
    n_col,
    border,
    hub,
    grads,
    rim,
    hub_total,
    weights,
    bias,
    hub_in,
    col_in,
    row_in,
    rim_send,
    rim_recv,
    hub_send,
    hub_recv,
    col_send,
    col_recv,
    row_send,
    row_recv,
    out_send,
    out_recv,
):
    row, col = lax.axis_index("row"), lax.axis_index("col")
    share = hub_total.shape[0]
    part = weights.shape[1]
    peers = [lax.rem(col + k, n_col) for k in range(1, n_col)]
    row_peers = [lax.rem(row + k, n_row) for k in range(1, n_row)]
    greet(row, col, row_peers, peers)

    def remote(src, dst, send, recv, device):
        return pltpu.make_async_remote_copy(
            src_ref=src,
            dst_ref=dst,
            send_sem=send,
            recv_sem=recv,
            device_id=device,
            device_id_type=MESH,
        )

    first = [
        remote(grads.at[peer], col_in.at[col], col_send.at[k], col_recv.at[k], (row, peer))
        for k, peer in enumerate(peers)
    ]
    for copy in first:
        copy.start()
    up, down = rim_copies(
        row,
        col,
        n_row,
        border.at[pl.ds(0, HALO)],
        border.at[pl.ds(HALO, HALO)],
        rim.at[pl.ds(HALO, HALO)],
        rim.at[pl.ds(0, HALO)],
        rim_send,
        rim_recv,
    )
    start_rims(row, n_row, up, down)
    sends = [
        remote(
            hub.at[pl.ds(pl.multiple_of(peer * share, share), share)],
            hub_in.at[col],
            hub_send.at[k],
            hub_recv.at[k],
            (row, peer),
        )
        for k, peer in enumerate(peers)
    ]
    for copy in sends:
        copy.start()

    @pl.when(row == 0)
    def _():
        rim[:HALO, :] = jnp.zeros((HALO, rim.shape[1]), rim.dtype)

    @pl.when(row == n_row - 1)
    def _():
        rim[HALO:, :] = jnp.zeros((HALO, rim.shape[1]), rim.dtype)

    col_in[col] = grads[col]
    for copy in first:
        copy.wait()
    total = col_in[0]
    for k in range(1, n_col):
        total = total + col_in[k]
    row_in[row] = total
    second = [
        remote(row_in.at[row], row_in.at[row], row_send.at[k], row_recv.at[k], (peer, col))
        for k, peer in enumerate(row_peers)
    ]
    for copy in second:
        copy.start()
    hub_in[col] = hub[pl.ds(pl.multiple_of(col * share, share), share), :]
    for copy in second:
        copy.wait()
    total = row_in[0]
    for k in range(1, n_row):
        total = total + row_in[k]
    weights[col] = total[:part]
    bias[...] = jnp.sum(total[part:], axis=0, keepdims=True)
    third = [
        remote(weights.at[col], weights.at[col], out_send.at[k], out_recv.at[k], (row, peer))
        for k, peer in enumerate(peers)
    ]
    for copy in third:
        copy.start()
    for copy in sends:
        copy.wait()
    shared = hub_in[0].astype(jnp.float32)
    for k in range(1, n_col):
        shared = shared + hub_in[k].astype(jnp.float32)
    hub_total[...] = shared
    for copy in third:
        copy.wait()
    finish_rims(row, n_row, up, down)


def exit_exchange(border, hub, grads, n_row, n_col):
    width = border.shape[1]
    share = hub.shape[0] // n_col
    part, hidden = grads.shape[1] - 8, grads.shape[2]
    vmem = pl.BlockSpec(memory_space=pltpu.VMEM)
    dma = pltpu.SemaphoreType.DMA
    return pl.pallas_call(
        functools.partial(exit_kernel, n_row, n_col),
        out_shape=(
            jax.ShapeDtypeStruct(border.shape, jnp.bfloat16),
            jax.ShapeDtypeStruct((share, width), jnp.float32),
            jax.ShapeDtypeStruct((n_col, part, hidden), jnp.float32),
            jax.ShapeDtypeStruct((1, hidden), jnp.float32),
        ),
        in_specs=[vmem] * 3,
        out_specs=(vmem,) * 4,
        scratch_shapes=[
            pltpu.VMEM((n_col, share, width), jnp.bfloat16),
            pltpu.VMEM(grads.shape, jnp.float32),
            pltpu.VMEM((n_row,) + grads.shape[1:], jnp.float32),
            dma((2,)),
            dma((2,)),
        ]
        + [dma((n_col - 1,))] * 4
        + [dma((n_row - 1,))] * 2
        + [dma((n_col - 1,))] * 2,
        compiler_params=pltpu.CompilerParams(
            collective_id=1, has_side_effects=True, vmem_limit_bytes=VMEM_LIMIT
        ),
        name="exit_exchange",
    )(border, hub, grads)


def finish_kernel(hub_rows, own, dz, w_self, rim, hub, out, total):
    chunk = 512
    nodes = own.shape[0]

    def back(i, carry):
        at = pl.ds(pl.multiple_of(i * chunk, chunk), chunk)
        total[at, :] = own[at, :] + lax.dot_general(
            dz[at, :], w_self[...], (((1,), (1,)), ((), ())), preferred_element_type=jnp.float32
        )
        return carry

    lax.fori_loop(0, nodes // chunk, back, 0)
    total[:HALO, :] += rim[:HALO, :].astype(jnp.float32)
    total[nodes - HALO :, :] += rim[HALO:, :].astype(jnp.float32)

    def add(i, carry):
        for u in range(UNROLL):
            k = i * UNROLL + u
            at = pl.ds(hub_rows[k], 1)
            total[at, :] += hub[pl.ds(k, 1), :]
        return carry

    lax.fori_loop(0, hub.shape[0] // UNROLL, add, 0)
    out[...] = total[...].astype(out.dtype)


def finish(hub_rows, own, dz, w_self, rim, hub):
    vmem = pl.BlockSpec(memory_space=pltpu.VMEM)
    return pl.pallas_call(
        finish_kernel,
        out_shape=jax.ShapeDtypeStruct(own.shape, jnp.bfloat16),
        in_specs=[pl.BlockSpec(memory_space=pltpu.SMEM)] + [vmem] * 5,
        out_specs=vmem,
        scratch_shapes=[pltpu.VMEM(own.shape, jnp.float32)],
        compiler_params=pltpu.CompilerParams(vmem_limit_bytes=VMEM_LIMIT),
        name="finish",
    )(hub_rows, own, dz, w_self, rim, hub)


def gelu_tanh(value):
    return jax.nn.gelu(value, approximate=True)


def on_device(features, neighbors, counts, hub_rows, w_self, w_neigh, out_bias, cotangent):
    node_count = features.shape[0]
    n_row, n_col = lax.axis_size("row"), lax.axis_size("col")
    lower, upper, hub_table = entry_exchange(features, hub_rows, n_row, n_col)
    hubs = hub_table.shape[0]
    rows = neighbors.T
    keys = counts * node_count + jnp.arange(node_count, dtype=jnp.int32)
    order = lax.sort(keys, is_stable=False) % node_count
    starts = jnp.sum(
        counts[None, :] <= jnp.arange(FANOUT + 1)[:, None], axis=1, dtype=jnp.int32
    )
    divisor = counts.astype(jnp.float32)[:, None]
    agg = (gather_sum(rows, starts, order, lower, features, upper, hub_table) / divisor).astype(jnp.bfloat16)
    pre = (
        jnp.dot(features, w_self, preferred_element_type=jnp.float32)
        + jnp.dot(agg, w_neigh, preferred_element_type=jnp.float32)
        + out_bias
    )
    act, backward = jax.vjp(gelu_tanh, pre)
    activations = act.astype(jnp.bfloat16)
    dz = backward(cotangent.astype(jnp.float32))[0].astype(jnp.bfloat16)
    dims = (((0,), (0,)), ((), ()))
    back_dims = (((1,), (1,)), ((), ()))
    grad_self = lax.dot_general(features, dz, dims, preferred_element_type=jnp.float32)
    grad_b = jnp.sum(dz.astype(jnp.float32), axis=0)
    grad_neigh = lax.dot_general(agg, dz, dims, preferred_element_type=jnp.float32)
    source = lax.dot_general(dz, w_neigh, back_dims, preferred_element_type=jnp.float32) / divisor
    mine, border, hub_grads = scatter_sum(rows, starts, order, source, hubs)
    hidden = dz.shape[1]
    blocks = jnp.concatenate([grad_self, grad_neigh], axis=0).reshape(n_col, -1, hidden)
    grads = jnp.concatenate([blocks, jnp.broadcast_to(jnp.pad(grad_b[None, :], ((0, 7), (0, 0))), (n_col, 8, hidden))], axis=1)
    rim, hub_share, weights, bias = exit_exchange(border, hub_grads, grads, n_row, n_col)
    grad_features = finish(hub_rows, mine, dz, w_self, rim, hub_share)
    weights = weights.reshape(2, -1, hidden)
    grad_self, grad_neigh, grad_b = weights[0], weights[1], bias[0]
    return (activations, grad_features, grad_self, grad_neigh, grad_b)


def solution(mesh):
    placed = (
        P(("row", "col"), None),
        P(("row", "col"), None),
        P(("row", "col")),
        P(("row", "col")),
        P(),
        P(),
        P(),
        P(("row", "col"), None),
    )
    return jax.shard_map(
        on_device,
        mesh=mesh,
        in_specs=placed,
        out_specs=(P(("row", "col"), None), P(("row", "col"), None), P(), P(), P()),
        check_vma=False,
    )
```

```python
import functools

import jax
import jax.numpy as jnp
from jax import lax
from jax.experimental import pallas as pl
from jax.experimental.pallas import tpu as pltpu
from jax.sharding import PartitionSpec as P

FANOUT = 10
HALO = 1024
UNROLL = 8
GROUPS = (32, 4, 1)
CHUNK = 256
VMEM_LIMIT = 60 * 1024 * 1024


def by_count(starts_ref, order_ref, visit):
    for live in range(1, FANOUT + 1):
        first, last = starts_ref[live - 1], starts_ref[live]
        for size in GROUPS:
            groups = lax.div(last - first, size)

            def group(i, carry, first=first, live=live, size=size):
                at = first + i * size
                visit([order_ref[at + u] for u in range(size)], live)
                return carry

            lax.fori_loop(0, groups, group, 0)
            first = first + groups * size


def layer_kernel(
    rows_ref,
    starts_ref,
    order_ref,
    lower_ref,
    own_ref,
    upper_ref,
    hub_ref,
    weights_ref,
    bias_ref,
    cotangent_ref,
    act_out,
    local_ref,
    border_ref,
    hub_grad_ref,
    grads_ref,
    table,
    held,
    cotangent,
    act,
    grad_w,
    grad_b,
    in_sem,
    out_sem,
    *sums,
):
    kinds = len(sums)
    extent, width = table.shape
    nodes = own_ref.shape[0]
    hidden = grad_w.shape[1]
    load = pltpu.make_async_copy(cotangent_ref, cotangent, in_sem)
    load.start()
    at = 0
    for part in (lower_ref, own_ref, upper_ref, hub_ref):
        size = part.shape[0]
        table[at : at + size, :] = part[...].astype(jnp.float32)
        at += size

    def gather(group, live):
        for n in group:
            picked = [table[pl.ds(rows_ref[s, n], 1), :] for s in range(live)]
            while len(picked) > 1:
                picked = [a + b for a, b in zip(picked[::2], picked[1::2])] + (
                    [picked[-1]] if len(picked) % 2 else []
                )
            held[pl.ds(n, 1), :] = picked[0] * (1.0 / live)

    by_count(starts_ref, order_ref, gather)

    load.wait()
    grad_w[...] = jnp.zeros_like(grad_w)
    grad_b[...] = jnp.zeros_like(grad_b)
    slope, cubic = 0.7978845608028654, 0.044715

    def dense(i, carry):
        at = pl.ds(pl.multiple_of(i * CHUNK, CHUNK), CHUNK)
        inputs = jnp.concatenate([own_ref[at, :], held[at, :].astype(jnp.bfloat16)], axis=1)
        z = (
            jnp.dot(inputs, weights_ref[...], preferred_element_type=jnp.float32) + bias_ref[...]
        )
        square = z * z
        tilt = jnp.tanh(slope * (z + cubic * (square * z)))
        half = 0.5 * (1.0 + tilt)
        act[at, :] = (z * half).astype(jnp.bfloat16)
        rise = half + 0.5 * z * ((1.0 - tilt * tilt) * (slope * (1.0 + 3.0 * cubic * square)))
        dz = (cotangent[at, :].astype(jnp.float32) * rise).astype(jnp.bfloat16)
        grad_w[...] += lax.dot_general(
            inputs, dz, (((0,), (0,)), ((), ())), preferred_element_type=jnp.float32
        )
        grad_b[...] += jnp.sum(dz.astype(jnp.float32).reshape(CHUNK // 8, 8, hidden), axis=0)
        back = lax.dot_general(
            dz, weights_ref[...], (((1,), (1,)), ((), ())), preferred_element_type=jnp.float32
        )
        local_ref[at, :] = back[:, :width]
        held[at, :] = back[:, width:]
        return carry

    lax.fori_loop(0, nodes // CHUNK, dense, 0)
    store = pltpu.make_async_copy(act, act_out, out_sem)
    store.start()
    blocks, part = grads_ref.shape[0], grads_ref.shape[1] - 8
    for k in range(blocks):
        grads_ref[k, :part, :] = grad_w[k * part : (k + 1) * part, :]
        grads_ref[k, part:, :] = grad_b[...]

    def clear(i, carry):
        for total in sums:
            total[pl.ds(pl.multiple_of(i * CHUNK, CHUNK), CHUNK), :] = jnp.zeros(
                (CHUNK, width), jnp.float32
            )
        return carry

    lax.fori_loop(0, extent // CHUNK, clear, 0)

    def scatter(group, live):
        values = [held[pl.ds(n, 1), :] * (1.0 / live) for n in group]
        edges = [(u, s) for u in range(len(group)) for s in range(live)]
        for first in range(0, len(edges), kinds):
            batch = edges[first : first + kinds]
            rows = [rows_ref[s, group[u]] for u, s in batch]
            old = [sums[k][pl.ds(row, 1), :] for k, row in enumerate(rows)]
            for k, (u, s) in enumerate(batch):
                sums[k][pl.ds(rows[k], 1), :] = old[k] + values[u]

    by_count(starts_ref, order_ref, scatter)

    def added(at, size):
        total = sums[0][pl.ds(at, size), :]
        for other in sums[1:]:
            total = total + other[pl.ds(at, size), :]
        return total

    def emit(ref, ref_at, at, count, more):
        def one(i, carry):
            off = pl.multiple_of(i * 128, 128)
            total = added(at + off, 128)
            if more:
                total = total + ref[pl.ds(ref_at + off, 128), :]
            ref[pl.ds(ref_at + off, 128), :] = total.astype(ref.dtype)
            return carry

        lax.fori_loop(0, count // 128, one, 0)

    emit(border_ref, 0, 0, HALO, False)
    emit(local_ref, 0, HALO, nodes, True)
    emit(border_ref, HALO, HALO + nodes, HALO, False)
    emit(hub_grad_ref, 0, 2 * HALO + nodes, hub_grad_ref.shape[0], False)
    store.wait()


def layer(rows, starts, order, lower, own, upper, hubs, weights, bias, cotangent, n_col):
    nodes, width = own.shape
    hidden = weights.shape[1]
    extent = lower.shape[0] + nodes + upper.shape[0] + hubs.shape[0]
    kinds = 10 if extent <= 8192 else 5
    vmem = pl.BlockSpec(memory_space=pltpu.VMEM)
    anywhere = pl.BlockSpec(memory_space=pl.ANY)
    return pl.pallas_call(
        layer_kernel,
        out_shape=(
            jax.ShapeDtypeStruct((nodes, hidden), jnp.bfloat16),
            jax.ShapeDtypeStruct((nodes, width), jnp.float32),
            jax.ShapeDtypeStruct((2 * HALO, width), jnp.bfloat16),
            jax.ShapeDtypeStruct(hubs.shape, jnp.bfloat16),
            jax.ShapeDtypeStruct((n_col, 2 * width // n_col + 8, hidden), jnp.float32),
        ),
        in_specs=[pl.BlockSpec(memory_space=pltpu.SMEM)] * 3 + [vmem] * 6 + [anywhere],
        out_specs=(anywhere, vmem, vmem, vmem, vmem),
        scratch_shapes=[
            pltpu.VMEM((extent, width), jnp.float32),
            pltpu.VMEM((nodes, width), jnp.float32),
            pltpu.VMEM((nodes, hidden), jnp.bfloat16),
            pltpu.VMEM((nodes, hidden), jnp.bfloat16),
            pltpu.VMEM((2 * width, hidden), jnp.float32),
            pltpu.VMEM((8, hidden), jnp.float32),
            pltpu.SemaphoreType.DMA,
            pltpu.SemaphoreType.DMA,
        ]
        + [pltpu.VMEM((extent, width), jnp.float32)] * kinds,
        compiler_params=pltpu.CompilerParams(vmem_limit_bytes=VMEM_LIMIT),
        name="layer",
    )(rows, starts, order, lower, own, upper, hubs, weights, bias, cotangent)


MESH = pl.DeviceIdType.MESH


def greet(row, col, row_peers, col_peers):
    barrier = pltpu.get_barrier_semaphore()
    for peer in row_peers:
        pl.semaphore_signal(barrier, inc=1, device_id=(peer, col), device_id_type=MESH)
    for peer in col_peers:
        pl.semaphore_signal(barrier, inc=1, device_id=(row, peer), device_id_type=MESH)
    pl.semaphore_wait(barrier, len(row_peers) + len(col_peers))


def rim_copies(row, col, n_row, head, tail, below, above, send, recv):
    up = pltpu.make_async_remote_copy(
        src_ref=tail,
        dst_ref=above,
        send_sem=send.at[0],
        recv_sem=recv.at[0],
        device_id=(lax.rem(row + 1, n_row), col),
        device_id_type=MESH,
    )
    down = pltpu.make_async_remote_copy(
        src_ref=head,
        dst_ref=below,
        send_sem=send.at[1],
        recv_sem=recv.at[1],
        device_id=(lax.rem(row + n_row - 1, n_row), col),
        device_id_type=MESH,
    )
    return up, down


def start_rims(row, n_row, up, down):
    pl.when(row < n_row - 1)(lambda: up.start())
    pl.when(row > 0)(lambda: down.start())


def finish_rims(row, n_row, up, down):
    @pl.when(row < n_row - 1)
    def _():
        up.wait_send()
        down.wait_recv()

    @pl.when(row > 0)
    def _():
        down.wait_send()
        up.wait_recv()


def entry_kernel(
    n_row,
    n_col,
    hub_rows,
    own,
    lower,
    upper,
    hubs,
    wide,
    picked,
    hub,
    own_sem,
    rim_send,
    rim_recv,
    hub_send,
    hub_recv,
):
    row, col = lax.axis_index("row"), lax.axis_index("col")
    nodes, share = own.shape[0], hub.shape[0]
    peers = [lax.rem(col + k, n_col) for k in range(1, n_col)]
    greet(row, col, [lax.rem(row + k, n_row) for k in range(1, n_row)], peers)
    up, down = rim_copies(
        row,
        col,
        n_row,
        own.at[pl.ds(0, HALO)],
        own.at[pl.ds(nodes - HALO, HALO)],
        upper,
        lower,
        rim_send,
        rim_recv,
    )
    start_rims(row, n_row, up, down)
    wide[...] = own[...].astype(jnp.float32)

    def pick(i, carry):
        for u in range(UNROLL):
            k = i * UNROLL + u
            picked[pl.ds(k, 1), :] = wide[pl.ds(hub_rows[k], 1), :]
        return carry

    lax.fori_loop(0, share // UNROLL, pick, 0)
    hub[...] = picked[...].astype(jnp.bfloat16)
    mine = hubs.at[pl.ds(pl.multiple_of(col * share, share), share)]
    copies = [
        pltpu.make_async_remote_copy(
            src_ref=hub,
            dst_ref=mine,
            send_sem=hub_send.at[k],
            recv_sem=hub_recv.at[k],
            device_id=(row, peer),
            device_id_type=MESH,
        )
        for k, peer in enumerate(peers)
    ]
    for copy in copies:
        copy.start()
    kept = pltpu.make_async_copy(hub, mine, own_sem)
    kept.start()
    kept.wait()
    for copy in copies:
        copy.wait()
    finish_rims(row, n_row, up, down)


def entry_exchange(features, hub_rows, n_row, n_col):
    width = features.shape[1]
    share = hub_rows.shape[0]
    anywhere = pl.BlockSpec(memory_space=pl.ANY)
    dma = pltpu.SemaphoreType.DMA
    return pl.pallas_call(
        functools.partial(entry_kernel, n_row, n_col),
        out_shape=(
            jax.ShapeDtypeStruct((HALO, width), jnp.bfloat16),
            jax.ShapeDtypeStruct((HALO, width), jnp.bfloat16),
            jax.ShapeDtypeStruct((n_col * share, width), jnp.bfloat16),
        ),
        in_specs=[
            pl.BlockSpec(memory_space=pltpu.SMEM),
            pl.BlockSpec(memory_space=pltpu.VMEM),
        ],
        out_specs=(anywhere,) * 3,
        scratch_shapes=[
            pltpu.VMEM(features.shape, jnp.float32),
            pltpu.VMEM((share, width), jnp.float32),
            pltpu.VMEM((share, width), jnp.bfloat16),
            dma,
            dma((2,)),
            dma((2,)),
            dma((n_col - 1,)),
            dma((n_col - 1,)),
        ],
        compiler_params=pltpu.CompilerParams(
            collective_id=0, has_side_effects=True, vmem_limit_bytes=VMEM_LIMIT
        ),
        name="entry_exchange",
    )(hub_rows, features)


def exit_kernel(
    n_row,
    n_col,
    border,
    hub,
    grads,
    rim,
    hub_total,
    weights,
    bias,
    hub_in,
    col_in,
    row_in,
    rim_send,
    rim_recv,
    hub_send,
    hub_recv,
    col_send,
    col_recv,
    row_send,
    row_recv,
    out_send,
    out_recv,
):
    row, col = lax.axis_index("row"), lax.axis_index("col")
    share = hub_total.shape[0]
    part = weights.shape[1]
    peers = [lax.rem(col + k, n_col) for k in range(1, n_col)]
    row_peers = [lax.rem(row + k, n_row) for k in range(1, n_row)]
    greet(row, col, row_peers, peers)

    def remote(src, dst, send, recv, device):
        return pltpu.make_async_remote_copy(
            src_ref=src,
            dst_ref=dst,
            send_sem=send,
            recv_sem=recv,
            device_id=device,
            device_id_type=MESH,
        )

    first = [
        remote(grads.at[peer], col_in.at[col], col_send.at[k], col_recv.at[k], (row, peer))
        for k, peer in enumerate(peers)
    ]
    for copy in first:
        copy.start()
    up, down = rim_copies(
        row,
        col,
        n_row,
        border.at[pl.ds(0, HALO)],
        border.at[pl.ds(HALO, HALO)],
        rim.at[pl.ds(HALO, HALO)],
        rim.at[pl.ds(0, HALO)],
        rim_send,
        rim_recv,
    )
    start_rims(row, n_row, up, down)
    sends = [
        remote(
            hub.at[pl.ds(pl.multiple_of(peer * share, share), share)],
            hub_in.at[col],
            hub_send.at[k],
            hub_recv.at[k],
            (row, peer),
        )
        for k, peer in enumerate(peers)
    ]
    for copy in sends:
        copy.start()

    @pl.when(row == 0)
    def _():
        rim[:HALO, :] = jnp.zeros((HALO, rim.shape[1]), rim.dtype)

    @pl.when(row == n_row - 1)
    def _():
        rim[HALO:, :] = jnp.zeros((HALO, rim.shape[1]), rim.dtype)

    col_in[col] = grads[col]
    for copy in first:
        copy.wait()
    total = col_in[0]
    for k in range(1, n_col):
        total = total + col_in[k]
    row_in[row] = total
    second = [
        remote(row_in.at[row], row_in.at[row], row_send.at[k], row_recv.at[k], (peer, col))
        for k, peer in enumerate(row_peers)
    ]
    for copy in second:
        copy.start()
    hub_in[col] = hub[pl.ds(pl.multiple_of(col * share, share), share), :]
    for copy in second:
        copy.wait()
    total = row_in[0]
    for k in range(1, n_row):
        total = total + row_in[k]
    weights[col] = total[:part]
    bias[...] = jnp.sum(total[part:], axis=0, keepdims=True)
    third = [
        remote(weights.at[col], weights.at[col], out_send.at[k], out_recv.at[k], (row, peer))
        for k, peer in enumerate(peers)
    ]
    for copy in third:
        copy.start()
    for copy in sends:
        copy.wait()
    shared = hub_in[0].astype(jnp.float32)
    for k in range(1, n_col):
        shared = shared + hub_in[k].astype(jnp.float32)
    hub_total[...] = shared
    for copy in third:
        copy.wait()
    finish_rims(row, n_row, up, down)


def exit_exchange(border, hub, grads, n_row, n_col):
    width = border.shape[1]
    share = hub.shape[0] // n_col
    part, hidden = grads.shape[1] - 8, grads.shape[2]
    vmem = pl.BlockSpec(memory_space=pltpu.VMEM)
    dma = pltpu.SemaphoreType.DMA
    return pl.pallas_call(
        functools.partial(exit_kernel, n_row, n_col),
        out_shape=(
            jax.ShapeDtypeStruct(border.shape, jnp.bfloat16),
            jax.ShapeDtypeStruct((share, width), jnp.float32),
            jax.ShapeDtypeStruct((n_col, part, hidden), jnp.float32),
            jax.ShapeDtypeStruct((1, hidden), jnp.float32),
        ),
        in_specs=[vmem] * 3,
        out_specs=(vmem,) * 4,
        scratch_shapes=[
            pltpu.VMEM((n_col, share, width), jnp.bfloat16),
            pltpu.VMEM(grads.shape, jnp.float32),
            pltpu.VMEM((n_row,) + grads.shape[1:], jnp.float32),
            dma((2,)),
            dma((2,)),
        ]
        + [dma((n_col - 1,))] * 4
        + [dma((n_row - 1,))] * 2
        + [dma((n_col - 1,))] * 2,
        compiler_params=pltpu.CompilerParams(
            collective_id=1, has_side_effects=True, vmem_limit_bytes=VMEM_LIMIT
        ),
        name="exit_exchange",
    )(border, hub, grads)


def finish_kernel(hub_rows, own, rim, hub, out, total):
    nodes = own.shape[0]
    total[...] = own[...]
    total[:HALO, :] += rim[:HALO, :].astype(jnp.float32)
    total[nodes - HALO :, :] += rim[HALO:, :].astype(jnp.float32)

    def add(i, carry):
        for u in range(UNROLL):
            k = i * UNROLL + u
            at = pl.ds(hub_rows[k], 1)
            total[at, :] += hub[pl.ds(k, 1), :]
        return carry

    lax.fori_loop(0, hub.shape[0] // UNROLL, add, 0)
    out[...] = total[...].astype(out.dtype)


def finish(hub_rows, own, rim, hub):
    vmem = pl.BlockSpec(memory_space=pltpu.VMEM)
    return pl.pallas_call(
        finish_kernel,
        out_shape=jax.ShapeDtypeStruct(own.shape, jnp.bfloat16),
        in_specs=[pl.BlockSpec(memory_space=pltpu.SMEM)] + [vmem] * 3,
        out_specs=vmem,
        scratch_shapes=[pltpu.VMEM(own.shape, jnp.float32)],
        compiler_params=pltpu.CompilerParams(vmem_limit_bytes=VMEM_LIMIT),
        name="finish",
    )(hub_rows, own, rim, hub)


def on_device(features, neighbors, counts, hub_rows, w_self, w_neigh, out_bias, cotangent):
    node_count = features.shape[0]
    n_row, n_col = lax.axis_size("row"), lax.axis_size("col")
    lower, upper, hub_table = entry_exchange(features, hub_rows, n_row, n_col)
    rows = neighbors.T
    keys = counts * node_count + jnp.arange(node_count, dtype=jnp.int32)
    order = lax.sort(keys, is_stable=False) % node_count
    starts = jnp.sum(
        counts[None, :] <= jnp.arange(FANOUT + 1)[:, None], axis=1, dtype=jnp.int32
    )
    stacked = jnp.concatenate([w_self, w_neigh], axis=0)
    activations, mine, border, hub_grads, grads = layer(
        rows,
        starts,
        order,
        lower,
        features,
        upper,
        hub_table,
        stacked,
        out_bias[None, :],
        cotangent,
        n_col,
    )
    rim, hub_share, weights, bias = exit_exchange(border, hub_grads, grads, n_row, n_col)
    grad_features = finish(hub_rows, mine, rim, hub_share)
    weights = weights.reshape(2, -1, weights.shape[2])
    grad_self, grad_neigh, grad_b = weights[0], weights[1], bias[0]
    return (activations, grad_features, grad_self, grad_neigh, grad_b)


def solution(mesh):
    placed = (
        P(("row", "col"), None),
        P(("row", "col"), None),
        P(("row", "col")),
        P(("row", "col")),
        P(),
        P(),
        P(),
        P(("row", "col"), None),
    )
    return jax.shard_map(
        on_device,
        mesh=mesh,
        in_specs=placed,
        out_specs=(P(("row", "col"), None), P(("row", "col"), None), P(), P(), P()),
        check_vma=False,
    )
```
